32 devices in a mesh: plate: 4 (over y, x), sub: 8 (over z, core).
Axes of the slice: x: 2, y: 2, z: 4, core: 2. Of those that a mesh axis runs over, the one named last changes fastest.
Arguments:
- populations: float32 [19, 16, 128, 128], P(None, 'plate', 'sub'), may hold values from 0.5 to 1.5
- solid: int32 [16, 128, 128], P('plate', 'sub'), may hold values 0 or 1
- marker_corner: int32 [3, 2048], P(None, ('plate', 'sub')), may hold values from 0 to 124, as said below
- marker_frac: float32 [3, 2048], P(None, ('plate', 'sub')), may hold values from 0 to 1
- marker_target: float32 [3, 2048], P(None, ('plate', 'sub')), may hold values from -0.6 to 0.6
- stiffness: float32 [2048], P(('plate', 'sub')), may hold values from 0.5 to 4
- displacement: float32 [3, 2048], P(None, ('plate', 'sub')), may hold values from -0.6 to 0.6
Outputs:
- populations_out: float32 [19, 16, 128, 128], P(None, 'plate', 'sub')
- displacement_out: float32 [3, 2048], P(None, ('plate', 'sub'))
- marker_force: float32 [3, 2048], P(None, ('plate', 'sub'))
The draws below stay inside these ranges and needn't reach their ends.
Inputs may be any that keep to these rules, and one draw needn't show every extreme that they name: `marker_corner`: components are the first cell of the stencil along the three dimensions. Every stencil lies inside the grid without wrapping, and along the first dimension inside the slab of 4 cells that its plate's markers share; the markers of plate p are rows p * 512 to (p + 1) * 512 - 1 and lie in slab p.
All inputs are finite; a program needn't handle non-finite values. No bound on the sum of `solid` on one device may be relied on, other than what follows from the above.
Results may differ from the reference program's by a relative error of at most 0.00011.
Values sent between devices are 32-bit elements; how exact they have to be, the bound alone decides.
A program may use at most 64 MiB of HBM per device.

```python
import math
import jax
import jax.numpy as jnp
from jax import lax

CX = 4
NZ = 128
M_DEV = 64
STEPS = 2
X = 16
Y = 128
MARKERS = 2048
N_PLATE = 4
N_SUB = 8


def draw_marker_corner(key, part):
    per_plate = M_DEV * N_SUB
    total = per_plate * N_PLATE
    y_band = max(Y // 4, 4)
    z_band = max(NZ // 2, 4)
    keys = jax.random.split(key, 5)
    plate_of = jnp.arange(total, dtype=jnp.int32) // per_plate
    y_first = jax.random.randint(keys[0], (N_PLATE,), 0, Y - y_band + 1).astype(jnp.int32)
    z_first = jax.random.randint(keys[1], (N_PLATE,), 0, NZ - z_band + 1).astype(jnp.int32)
    y_first = y_first.at[0].set(0).at[N_PLATE - 1].set(Y - y_band)
    z_first = z_first.at[0].set(0).at[N_PLATE - 1].set(NZ - z_band)
    x_off = jax.random.randint(keys[2], (total,), 0, CX - 3).astype(jnp.int32)
    y_off = jax.random.randint(keys[3], (total,), 0, y_band - 3).astype(jnp.int32)
    z_off = jax.random.randint(keys[4], (total,), 0, z_band - 3).astype(jnp.int32)
    x_off = x_off.at[0].set(0).at[total - 1].set(CX - 4)
    y_off = y_off.at[0].set(0).at[total - 1].set(y_band - 4)
    z_off = z_off.at[0].set(0).at[total - 1].set(z_band - 4)
    x_pos = plate_of * CX + x_off
    y_pos = y_first[plate_of] + y_off
    z_pos = z_first[plate_of] + z_off
    return jnp.stack([x_pos, y_pos, z_pos]).astype(jnp.int32)


def set_ends(entries, key, low, high):
    index_at = [jax.random.randint(jax.random.fold_in(key, axis), (), 0, length) for axis, length in enumerate(entries.shape)]
    widest = entries.shape.index(max(entries.shape))
    next_to = index_at[:widest] + [(index_at[widest] + 1) % entries.shape[widest]] + index_at[widest + 1:]
    return entries.at[tuple(index_at)].set(low).at[tuple(next_to)].set(high)


def block_scale(key, dims, cuts, smallest, top_value):
    level = 1.0
    for position, blocks in cuts:
        heights = jax.random.uniform(jax.random.fold_in(jax.random.fold_in(key, 6), position), (blocks,), jnp.float32, smallest / len(cuts), top_value / len(cuts))
        level = level * jnp.repeat(jnp.exp(heights), dims[position] // blocks).reshape((-1,) + (1,) * (len(dims) - 1 - position))
    return level


def normal_values(key, shape, scale, bound, shards=(), kind=jnp.bfloat16):
    values = scale * jax.random.normal(key, shape, jnp.float32)
    if shards:
        values = values * block_scale(key, shape, shards, -0.22, 0.18)
    return jnp.clip(values, -bound, bound).astype(kind)


def setup_inputs(seed: int = 0) -> dict:
    splits = jax.random.split(jax.random.key(seed), 8)
    return {
        "populations": jnp.clip(0.5 + 1.0 * jax.random.uniform(splits[0], (19, X, Y, NZ), jnp.float32) ** block_scale(splits[0], (19, X, Y, NZ), ((1, 4), (2, 8)), -0.2, 0.2), 0.5, 1.5),
        "solid": set_ends((jax.random.randint(splits[1], (X, Y, NZ), 0, 8) < 1).astype(jnp.int32), jax.random.fold_in(splits[1], 1), 0, 1),
        "marker_corner": draw_marker_corner(jax.random.fold_in(splits[7], 71), 0),
        "marker_frac": jnp.clip(1.0 * jax.random.uniform(splits[3], (3, MARKERS), jnp.float32) ** block_scale(splits[3], (3, MARKERS), ((1, 32),), -0.2, 0.2), 0.0, 1.0),
        "marker_target": normal_values(splits[4], (3, MARKERS), 0.1, 0.6, ((1, 32),), jnp.float32),
        "stiffness": jnp.clip(jnp.exp(math.log(4.0) - 2.0794415 * jax.random.uniform(splits[5], (MARKERS,), jnp.float32) ** block_scale(splits[5], (MARKERS,), ((0, 32),), -0.2, 0.2)), 0.5, 4.0),
        "displacement": normal_values(splits[6], (3, MARKERS), 0.1, 0.6, ((1, 32),), jnp.float32),
    }


DIRS = [(0, 0, 0), (1, 0, 0), (-1, 0, 0), (0, 1, 0), (0, -1, 0), (0, 0, 1), (0, 0, -1), (1, 1, 0), (-1, -1, 0), (1, -1, 0), (-1, 1, 0), (1, 0, 1), (-1, 0, -1), (1, 0, -1), (-1, 0, 1), (0, 1, 1), (0, -1, -1), (0, 1, -1), (0, -1, 1)]
WEIGHTS = [1.0 / 3.0] + [1.0 / 18.0] * 6 + [1.0 / 36.0] * 12
OPPOSITE = [0, 2, 1, 4, 3, 6, 5, 8, 7, 10, 9, 12, 11, 14, 13, 16, 15, 18, 17]
KAPPA = 4.0
RELAX = 0.9

def kernel_weights(frac):
    root = jnp.sqrt(1.0 + 4.0 * frac - 4.0 * frac * frac)
    second = (3.0 - 2.0 * frac + root) / 8.0
    third = (1.0 + 2.0 * frac + root) / 8.0
    return jnp.stack([0.5 - third, second, third, 0.5 - second])

def moments(pops):
    density = lax.optimization_barrier(jnp.sum(pops, 0))
    comps = []
    for axis in range(3):
        total = jnp.zeros_like(density)
        for index in range(19):
            if DIRS[index][axis] == 1:
                total = total + pops[index]
            elif DIRS[index][axis] == -1:
                total = total - pops[index]
        comps.append(total)
    return (density, jnp.stack(comps) / density)

def dotted(index, vectors):
    total = jnp.zeros_like(vectors[0])
    for axis in range(3):
        if DIRS[index][axis] == 1:
            total = total + vectors[axis]
        elif DIRS[index][axis] == -1:
            total = total - vectors[axis]
    return total

def collide(pops, density, velocity, spread, fluid):
    speed_sq = lax.optimization_barrier(jnp.sum(velocity * velocity, 0))
    result = []
    for index in range(19):
        proj = dotted(index, velocity)
        equil = WEIGHTS[index] * density * (1.0 + 3.0 * proj + 4.5 * proj * proj - 1.5 * speed_sq)
        post = pops[index] - (pops[index] - equil) / RELAX + 3.0 * WEIGHTS[index] * dotted(index, spread)
        result.append(jnp.where(fluid, post, pops[OPPOSITE[index]]))
    return jnp.stack(result)

def reference(populations, solid, marker_corner, marker_frac, marker_target, stiffness, displacement):
    x_weights = kernel_weights(marker_frac[0])
    y_weights = kernel_weights(marker_frac[1])
    z_weights = kernel_weights(marker_frac[2])
    fluid = solid == 0
    disp = displacement
    force = jnp.zeros_like(displacement)
    pops = populations
    for step in range(STEPS):
        density, velocity = moments(pops)
        marker_vel = jnp.zeros_like(displacement)
        for dx in range(4):
            for dy in range(4):
                for dz in range(4):
                    factor = x_weights[dx] * y_weights[dy] * z_weights[dz]
                    picked = velocity[:, marker_corner[0] + dx, marker_corner[1] + dy, marker_corner[2] + dz]
                    marker_vel = marker_vel + factor[None] * picked
        force = KAPPA * (marker_target - marker_vel) - stiffness[None] * disp
        disp = disp + marker_vel
        spread = jnp.zeros_like(velocity)
        for dx in range(4):
            for dy in range(4):
                for dz in range(4):
                    factor = x_weights[dx] * y_weights[dy] * z_weights[dz]
                    spread = spread.at[:, marker_corner[0] + dx, marker_corner[1] + dy, marker_corner[2] + dz].add(factor[None] * force)
        post = collide(pops, density, velocity, spread, fluid)
        pops = jnp.stack([jnp.roll(post[index], DIRS[index], axis=(0, 1, 2)) for index in range(19)])
    return (pops, disp, force)
```

```python
import functools

import jax
import jax.numpy as jnp
from jax import lax
from jax.experimental import pallas as pl
from jax.experimental.pallas import tpu as pltpu
from jax.sharding import PartitionSpec as P

STEPS = 2
DIRS = [
    (0, 0, 0),
    (1, 0, 0),
    (-1, 0, 0),
    (0, 1, 0),
    (0, -1, 0),
    (0, 0, 1),
    (0, 0, -1),
    (1, 1, 0),
    (-1, -1, 0),
    (1, -1, 0),
    (-1, 1, 0),
    (1, 0, 1),
    (-1, 0, -1),
    (1, 0, -1),
    (-1, 0, 1),
    (0, 1, 1),
    (0, -1, -1),
    (0, 1, -1),
    (0, -1, 1),
]
WEIGHTS = [1.0 / 3.0] + [1.0 / 18.0] * 6 + [1.0 / 36.0] * 12
PAIRS = [(i, i + 1) for i in range(1, 19, 2)]
KAPPA = 4.0
RELAX = 0.9
MESH = pl.DeviceIdType.MESH

X_UP = [i for i in range(19) if DIRS[i][0] == 1]
X_DN = [i for i in range(19) if DIRS[i][0] == -1]
Y_UP = [i for i in range(19) if DIRS[i][1] == 1]
Y_DN = [i for i in range(19) if DIRS[i][1] == -1]
EDGES = [i for i in range(19) if DIRS[i][0] and DIRS[i][1]]
ORDER = X_UP + X_DN + [i for i in range(19) if DIRS[i][0] == 0]
SLOT = [ORDER.index(i) for i in range(19)]


def signed_sum(index, vectors):
    total = None
    for axis in range(3):
        sign = DIRS[index][axis]
        if sign == 0:
            continue
        if total is None:
            total = vectors[axis] if sign == 1 else -vectors[axis]
        else:
            total = total + vectors[axis] if sign == 1 else total - vectors[axis]
    return total


def kernel_weights(frac):
    root = jnp.sqrt(1.0 + 4.0 * frac - 4.0 * frac * frac)
    second = (3.0 - 2.0 * frac + root) / 8.0
    third = (1.0 + 2.0 * frac + root) / 8.0
    return (0.5 - third, second, third, 0.5 - second)


def dense_rows(first, weights, length):
    cells = lax.broadcasted_iota(jnp.int32, (length, first.shape[1]), 0)
    offset = cells - first
    result = jnp.zeros(offset.shape, jnp.float32)
    for k in range(4):
        result = jnp.where(offset == k, weights[k], result)
    return result


def split(x):
    high = x.astype(jnp.bfloat16)
    return high, (x - high.astype(jnp.float32)).astype(jnp.bfloat16)


def dot3(a, b, dims):
    dot = functools.partial(
        lax.dot_general, dimension_numbers=(dims, ((), ())), preferred_element_type=jnp.float32
    )
    return dot(a[0], b[0]) + dot(a[1], b[0]) + dot(a[0], b[1])


def body(
    n_plate,
    n_sub,
    pops_ref,
    solid_ref,
    corner_ref,
    frac_ref,
    target_ref,
    stiff_ref,
    disp_ref,
    out_ref,
    disp_out,
    force_out,
    marks,
    velsum,
    post,
    mid,
    x_recv,
    y_send,
    y_recv,
    e_send,
    e_recv,
    own,
    mark_s,
    mark_r,
    vel_s,
    vel_r,
    halo_s,
    halo_r,
):
    _, nx, ny, nz = pops_ref.shape
    count = frac_ref.shape[1]
    lanes = 2 * count
    plate, me = lax.axis_index("plate"), lax.axis_index("sub")

    def at(d_plate, d_sub):
        return (lax.rem(plate + d_plate + n_plate, n_plate), lax.rem(me + d_sub + n_sub, n_sub))

    targets = [(1, 0), (-1, 0), (0, 1), (0, -1)] + [DIRS[i][:2] for i in EDGES]
    greeted = {(0, k) for k in range(1, n_sub)}
    greeted |= {(a % n_plate, b % n_sub) for a, b in targets}
    greeted = sorted(greeted)
    barrier = pltpu.get_barrier_semaphore()
    for a, b in greeted:
        pl.semaphore_signal(barrier, inc=1, device_id=at(a, b), device_id_type=MESH)

    right_half = jnp.zeros((8, lanes), jnp.float32)
    own[...] = right_half
    own[0:3, 0:count] = corner_ref[...].astype(jnp.float32)
    own[3:6, 0:count] = disp_ref[...]
    right_half = pltpu.roll(own[...], count, 1)
    own[0:3, 0:count] = frac_ref[...]
    own[3:6, 0:count] = target_ref[...]
    own[6:7, 0:count] = stiff_ref[...]
    left = lax.broadcasted_iota(jnp.int32, (8, lanes), 1) < count
    marks[me] = jnp.where(left, own[...], right_half)

    pl.semaphore_wait(barrier, len(greeted))

    def to_all(buffer, send, recv):
        copies = []
        for k in range(1, n_sub):
            copy = pltpu.make_async_remote_copy(
                src_ref=buffer.at[me],
                dst_ref=buffer.at[me],
                send_sem=send.at[k],
                recv_sem=recv.at[k],
                device_id=at(0, k),
                device_id_type=MESH,
            )
            copy.start()
            copies.append(copy)
        return copies

    def all_here(buffer, send, recv):
        for k in range(1, n_sub):
            slot = lax.rem(me - k + n_sub, n_sub)
            pltpu.make_async_remote_copy(
                src_ref=buffer.at[slot],
                dst_ref=buffer.at[slot],
                send_sem=send.at[k],
                recv_sem=recv.at[k],
                device_id=at(0, k),
                device_id_type=MESH,
            ).wait_recv()

    sent = to_all(marks, mark_s, mark_r)

    def moments(pops):
        density = pops[0]
        for i in range(1, 19):
            density = density + pops[i]
        comps = []
        for axis in range(3):
            total = jnp.zeros_like(density)
            for i in range(19):
                if DIRS[i][axis] == 1:
                    total = total + pops[i]
                elif DIRS[i][axis] == -1:
                    total = total - pops[i]
            comps.append(total)
        inverse = 1.0 / density
        return density, [c * inverse for c in comps]

    fluid = solid_ref[...] == 0
    keep = 1.0 - 1.0 / RELAX
    row = lax.broadcasted_iota(jnp.int32, (nx, ny, nz), 1)
    disp = None
    for step in range(STEPS):
        source = pops_ref if step == 0 else mid
        density, velocity = moments([source[i] for i in range(19)])
        flat = split(jnp.concatenate(velocity, 0).reshape(3 * nx * ny, nz))
        if step == 0:
            all_here(marks, mark_s, mark_r)
            firsts, seconds = [], []
            for pair in range(n_sub // 2):
                a, b = marks[2 * pair], marks[2 * pair + 1]
                firsts.append(jnp.where(left, a, pltpu.roll(b, count, 1)))
                seconds.append(jnp.where(left, pltpu.roll(a, count, 1), b))
            first, second = jnp.concatenate(firsts, 1), jnp.concatenate(seconds, 1)
            total = first.shape[1]
            corners = second[0:3].astype(jnp.int32)
            x_first = corners[0:1] - plate * nx
            y_first = corners[1:2] - me * ny
            x_w, y_w, z_w = [kernel_weights(first[k : k + 1]) for k in range(3)]
            y_rows = dense_rows(y_first, y_w, ny)
            planes = []
            for x in range(nx):
                w = jnp.zeros_like(x_w[0])
                for k in range(4):
                    w = jnp.where(x_first == x - k, x_w[k], w)
                planes.append(w * y_rows)
            xy_rows = jnp.concatenate(planes, 0)
            z_rows = split(dense_rows(corners[2:3], z_w, nz))
            target = [first[3 + k : 4 + k] for k in range(3)]
            spring = first[6:7]
            disp = [second[3 + k : 4 + k] for k in range(3)]
        along = dot3(flat, z_rows, ((1,), (0,)))
        cells = nx * ny
        partial = [
            jnp.sum(along[k * cells : (k + 1) * cells] * xy_rows, 0, keepdims=True)
            for k in range(3)
        ]
        velsum[step, me] = jnp.concatenate(partial, 1)
        sent += to_all(velsum.at[step], vel_s.at[step], vel_r.at[step])

        speed = velocity[0] * velocity[0] + velocity[1] * velocity[1] + velocity[2] * velocity[2]
        scaled = density * (1.0 / RELAX)
        base = scaled * (1.0 - 1.5 * speed)
        rest = source[0]
        post[step, SLOT[0]] = jnp.where(fluid, keep * rest + WEIGHTS[0] * base, rest)
        for i, j in PAIRS:
            proj = signed_sum(i, velocity)
            flow = scaled * proj
            even = WEIGHTS[i] * (base + 4.5 * flow * proj)
            odd = (3.0 * WEIGHTS[i]) * flow
            a, b = source[i], source[j]
            post[step, SLOT[i]] = jnp.where(fluid, keep * a + (even + odd), b)
            post[step, SLOT[j]] = jnp.where(fluid, keep * b + (even - odd), a)

        all_here(velsum.at[step], vel_s.at[step], vel_r.at[step])
        summed = velsum[step, 0]
        for s in range(1, n_sub):
            summed = summed + velsum[step, s]
        moved = [summed[:, k * total : (k + 1) * total] for k in range(3)]
        force = [KAPPA * (target[k] - moved[k]) - spring * disp[k] for k in range(3)]
        disp = [disp[k] + moved[k] for k in range(3)]
        weighted = split(jnp.concatenate([xy_rows * force[k] for k in range(3)], 0))
        spread = dot3(weighted, z_rows, ((1,), (1,))).reshape(3, nx, ny, nz)
        spread = [jnp.where(fluid, spread[k], 0.0) for k in range(3)]
        for i, j in PAIRS:
            push = (3.0 * WEIGHTS[i]) * signed_sum(i, spread)
            post[step, SLOT[i]] = post[step, SLOT[i]] + push
            post[step, SLOT[j]] = post[step, SLOT[j]] - push

        for n, i in enumerate(Y_UP):
            y_send[step, 0, n] = post[step, SLOT[i], :, ny - 1 : ny, :]
        for n, i in enumerate(Y_DN):
            y_send[step, 1, n] = post[step, SLOT[i], :, 0:1, :]
        for n, i in enumerate(EDGES):
            x = nx - 1 if DIRS[i][0] == 1 else 0
            y = ny - 1 if DIRS[i][1] == 1 else 0
            e_send[step, n] = post[step, SLOT[i], x, y : y + 1, :]
        ends = [
            (post.at[step, pl.ds(0, len(X_UP)), nx - 1], x_recv.at[step, 0]),
            (post.at[step, pl.ds(len(X_UP), len(X_DN)), 0], x_recv.at[step, 1]),
            (y_send.at[step, 0], y_recv.at[step, 0]),
            (y_send.at[step, 1], y_recv.at[step, 1]),
        ] + [(e_send.at[step, n], e_recv.at[step, n]) for n in range(len(EDGES))]
        halo = []
        for n, ((src, dst), (a, b)) in enumerate(zip(ends, targets)):
            copy = pltpu.make_async_remote_copy(
                src_ref=src,
                dst_ref=dst,
                send_sem=halo_s.at[step, n],
                recv_sem=halo_r.at[step, n],
                device_id=at(a, b),
                device_id_type=MESH,
            )
            copy.start()
            halo.append(copy)
        sent += halo

        dest = mid if step < STEPS - 1 else out_ref
        inner = [i for i in range(19) if not (DIRS[i][0] or DIRS[i][1])]
        for i in inner + [i for i in range(19) if i not in inner]:
            if i == 1:
                for copy in halo:
                    copy.wait_recv()
            dx, dy, dz = DIRS[i]
            cells_i = post[step, SLOT[i]]
            if dx == 1:
                cells_i = jnp.concatenate(
                    [x_recv[step, 0, X_UP.index(i)][None], cells_i[: nx - 1]], 0
                )
            elif dx == -1:
                cells_i = jnp.concatenate([cells_i[1:], x_recv[step, 1, X_DN.index(i)][None]], 0)
            if dy:
                side, names = (0, Y_UP) if dy == 1 else (1, Y_DN)
                edge = y_recv[step, side, names.index(i)]
                if dx == 1:
                    edge = jnp.concatenate(
                        [e_recv[step, EDGES.index(i)][None], edge[: nx - 1]], 0
                    )
                elif dx == -1:
                    edge = jnp.concatenate([edge[1:], e_recv[step, EDGES.index(i)][None]], 0)
                turned = pltpu.roll(cells_i, dy % ny, 1)
                cells_i = jnp.where(row == (0 if dy == 1 else ny - 1), edge, turned)
            if dz:
                cells_i = pltpu.roll(cells_i, dz % nz, 2)
            dest[i] = cells_i

    for values, result in ((disp, disp_out), (force, force_out)):
        for k in range(3):
            mine = jnp.zeros((1, lanes), jnp.float32)
            for pair in range(n_sub // 2):
                part = values[k][:, pair * lanes : (pair + 1) * lanes]
                mine = jnp.where(me // 2 == pair, part, mine)
            mine = jnp.where(lax.rem(me, 2) == 0, mine, pltpu.roll(mine, count, 1))
            result[k : k + 1, :] = mine[:, :count]
    for copy in sent:
        copy.wait_send()


def shards(n_plate, n_sub, populations, solid, corner, frac, target, stiffness, displacement):
    _, nx, ny, nz = populations.shape
    count = stiffness.shape[0]
    f32 = jnp.float32
    vmem = pl.BlockSpec(memory_space=pltpu.VMEM)
    total = count * n_sub
    faces = len(X_UP)
    return pl.pallas_call(
        functools.partial(body, n_plate, n_sub),
        out_shape=(
            jax.ShapeDtypeStruct(populations.shape, f32),
            jax.ShapeDtypeStruct(displacement.shape, f32),
            jax.ShapeDtypeStruct(displacement.shape, f32),
        ),
        in_specs=[vmem] * 7,
        out_specs=(vmem,) * 3,
        scratch_shapes=[
            pltpu.VMEM((n_sub, 8, 2 * count), f32),
            pltpu.VMEM((STEPS, n_sub, 1, 3 * total), f32),
            pltpu.VMEM((STEPS, 19, nx, ny, nz), f32),
            pltpu.VMEM((19, nx, ny, nz), f32),
            pltpu.VMEM((STEPS, 2, faces, ny, nz), f32),
            pltpu.VMEM((STEPS, 2, faces, nx, 1, nz), f32),
            pltpu.VMEM((STEPS, 2, faces, nx, 1, nz), f32),
            pltpu.VMEM((STEPS, len(EDGES), 1, nz), f32),
            pltpu.VMEM((STEPS, len(EDGES), 1, nz), f32),
            pltpu.VMEM((8, 2 * count), f32),
            pltpu.SemaphoreType.DMA((n_sub,)),
            pltpu.SemaphoreType.DMA((n_sub,)),
            pltpu.SemaphoreType.DMA((STEPS, n_sub)),
            pltpu.SemaphoreType.DMA((STEPS, n_sub)),
            pltpu.SemaphoreType.DMA((STEPS, 8)),
            pltpu.SemaphoreType.DMA((STEPS, 8)),
        ],
        compiler_params=pltpu.CompilerParams(
            collective_id=0, has_side_effects=True, vmem_limit_bytes=40 * 1024 * 1024
        ),
    )(populations, solid, corner, frac, target, stiffness[None], displacement)


def solution(mesh):
    in_specs = (
        P(None, "plate", "sub", None),
        P("plate", "sub", None),
        P(None, ("plate", "sub")),
        P(None, ("plate", "sub")),
        P(None, ("plate", "sub")),
        P(("plate", "sub")),
        P(None, ("plate", "sub")),
    )
    out_specs = (
        P(None, "plate", "sub", None),
        P(None, ("plate", "sub")),
        P(None, ("plate", "sub")),
    )
    run = functools.partial(shards, mesh.shape["plate"], mesh.shape["sub"])
    return jax.shard_map(run, mesh=mesh, in_specs=in_specs, out_specs=out_specs, check_vma=False)
```

```python
import functools

import jax
import jax.numpy as jnp
from jax import lax
from jax.experimental import pallas as pl
from jax.experimental.pallas import tpu as pltpu
from jax.sharding import PartitionSpec as P

STEPS = 2
DIRS = [
    (0, 0, 0),
    (1, 0, 0),
    (-1, 0, 0),
    (0, 1, 0),
    (0, -1, 0),
    (0, 0, 1),
    (0, 0, -1),
    (1, 1, 0),
    (-1, -1, 0),
    (1, -1, 0),
    (-1, 1, 0),
    (1, 0, 1),
    (-1, 0, -1),
    (1, 0, -1),
    (-1, 0, 1),
    (0, 1, 1),
    (0, -1, -1),
    (0, 1, -1),
    (0, -1, 1),
]
WEIGHTS = [1.0 / 3.0] + [1.0 / 18.0] * 6 + [1.0 / 36.0] * 12
PAIRS = [(i, i + 1) for i in range(1, 19, 2)]
KAPPA = 4.0
RELAX = 0.9
MESH = pl.DeviceIdType.MESH

X_UP = [i for i in range(19) if DIRS[i][0] == 1]
X_DN = [i for i in range(19) if DIRS[i][0] == -1]
Y_UP = [i for i in range(19) if DIRS[i][1] == 1]
Y_DN = [i for i in range(19) if DIRS[i][1] == -1]
EDGES = [i for i in range(19) if DIRS[i][0] and DIRS[i][1]]
ORDER = X_UP + X_DN + [i for i in range(19) if DIRS[i][0] == 0]
SLOT = [ORDER.index(i) for i in range(19)]


def signed_sum(index, vectors):
    total = None
    for axis in range(3):
        sign = DIRS[index][axis]
        if sign == 0:
            continue
        if total is None:
            total = vectors[axis] if sign == 1 else -vectors[axis]
        else:
            total = total + vectors[axis] if sign == 1 else total - vectors[axis]
    return total


def kernel_weights(frac):
    root = jnp.sqrt(1.0 + 4.0 * frac - 4.0 * frac * frac)
    second = (3.0 - 2.0 * frac + root) / 8.0
    third = (1.0 + 2.0 * frac + root) / 8.0
    return (0.5 - third, second, third, 0.5 - second)


def dense_rows(first, weights, length):
    cells = lax.broadcasted_iota(jnp.int32, (length, first.shape[1]), 0)
    offset = cells - first
    result = jnp.zeros(offset.shape, jnp.float32)
    for k in range(4):
        result = jnp.where(offset == k, weights[k], result)
    return result


def split(x):
    high = x.astype(jnp.bfloat16)
    return high, (x - high.astype(jnp.float32)).astype(jnp.bfloat16)


def dot3(a, b, dims):
    dot = functools.partial(
        lax.dot_general, dimension_numbers=(dims, ((), ())), preferred_element_type=jnp.float32
    )
    return dot(a[0], b[0]) + dot(a[1], b[0]) + dot(a[0], b[1])


def body(
    n_plate,
    n_sub,
    pops_hbm,
    solid_hbm,
    corner_hbm,
    frac_hbm,
    target_hbm,
    stiff_hbm,
    disp_hbm,
    out_ref,
    disp_out,
    force_out,
    pops_ref,
    solid_ref,
    corner_ref,
    frac_ref,
    target_ref,
    stiff_ref,
    disp_ref,
    marks,
    velsum,
    post,
    mid,
    x_recv,
    y_send,
    y_recv,
    e_send,
    e_recv,
    own,
    mark_s,
    mark_r,
    vel_s,
    vel_r,
    halo_s,
    halo_r,
    local,
):
    _, nx, ny, nz = pops_ref.shape
    count = frac_ref.shape[1]
    lanes = 2 * count
    plate, me = lax.axis_index("plate"), lax.axis_index("sub")

    def at(d_plate, d_sub):
        return (lax.rem(plate + d_plate + n_plate, n_plate), lax.rem(me + d_sub + n_sub, n_sub))

    targets = [(1, 0), (-1, 0), (0, 1), (0, -1)] + [DIRS[i][:2] for i in EDGES]
    greeted = {(0, k) for k in range(1, n_sub)}
    greeted |= {(a % n_plate, b % n_sub) for a, b in targets}
    greeted = sorted(greeted)
    barrier = pltpu.get_barrier_semaphore()
    for a, b in greeted:
        pl.semaphore_signal(barrier, inc=1, device_id=at(a, b), device_id_type=MESH)

    loads = [
        pltpu.make_async_copy(src, dst, local.at[n])
        for n, (src, dst) in enumerate(
            (
                (corner_hbm, corner_ref),
                (disp_hbm, disp_ref),
                (frac_hbm, frac_ref),
                (target_hbm, target_ref),
                (stiff_hbm, stiff_ref),
                (pops_hbm, pops_ref),
                (solid_hbm, solid_ref),
            )
        )
    ]
    for load in loads:
        load.start()
    for load in loads[:5]:
        load.wait()

    right_half = jnp.zeros((8, lanes), jnp.float32)
    own[...] = right_half
    own[0:3, 0:count] = corner_ref[...].astype(jnp.float32)
    own[3:6, 0:count] = disp_ref[...]
    right_half = pltpu.roll(own[...], count, 1)
    own[0:3, 0:count] = frac_ref[...]
    own[3:6, 0:count] = target_ref[...]
    own[6:7, 0:count] = stiff_ref[...]
    left = lax.broadcasted_iota(jnp.int32, (8, lanes), 1) < count
    marks[me] = jnp.where(left, own[...], right_half)

    pl.semaphore_wait(barrier, len(greeted))

    def to_all(buffer, send, recv):
        copies = []
        for k in range(1, n_sub):
            copy = pltpu.make_async_remote_copy(
                src_ref=buffer.at[me],
                dst_ref=buffer.at[me],
                send_sem=send.at[k],
                recv_sem=recv.at[k],
                device_id=at(0, k),
                device_id_type=MESH,
            )
            copy.start()
            copies.append(copy)
        return copies

    def all_here(buffer, send, recv):
        for k in range(1, n_sub):
            slot = lax.rem(me - k + n_sub, n_sub)
            pltpu.make_async_remote_copy(
                src_ref=buffer.at[slot],
                dst_ref=buffer.at[slot],
                send_sem=send.at[k],
                recv_sem=recv.at[k],
                device_id=at(0, k),
                device_id_type=MESH,
            ).wait_recv()

    sent = to_all(marks, mark_s, mark_r)

    def moments(pops):
        density = pops[0]
        for i in range(1, 19):
            density = density + pops[i]
        comps = []
        for axis in range(3):
            total = jnp.zeros_like(density)
            for i in range(19):
                if DIRS[i][axis] == 1:
                    total = total + pops[i]
                elif DIRS[i][axis] == -1:
                    total = total - pops[i]
            comps.append(total)
        inverse = 1.0 / density
        return density, [c * inverse for c in comps]

    for load in loads[5:]:
        load.wait()
    fluid = solid_ref[...] == 0
    keep = 1.0 - 1.0 / RELAX
    row = lax.broadcasted_iota(jnp.int32, (nx, ny, nz), 1)
    disp = None
    for step in range(STEPS):
        source = pops_ref if step == 0 else mid
        density, velocity = moments([source[i] for i in range(19)])
        flat = split(jnp.concatenate(velocity, 0).reshape(3 * nx * ny, nz))
        if step == 0:
            all_here(marks, mark_s, mark_r)
            firsts, seconds = [], []
            for pair in range(n_sub // 2):
                a, b = marks[2 * pair], marks[2 * pair + 1]
                firsts.append(jnp.where(left, a, pltpu.roll(b, count, 1)))
                seconds.append(jnp.where(left, pltpu.roll(a, count, 1), b))
            first, second = jnp.concatenate(firsts, 1), jnp.concatenate(seconds, 1)
            total = first.shape[1]
            corners = second[0:3].astype(jnp.int32)
            x_first = corners[0:1] - plate * nx
            y_first = corners[1:2] - me * ny
            x_w, y_w, z_w = [kernel_weights(first[k : k + 1]) for k in range(3)]
            y_rows = dense_rows(y_first, y_w, ny)
            planes = []
            for x in range(nx):
                w = jnp.zeros_like(x_w[0])
                for k in range(4):
                    w = jnp.where(x_first == x - k, x_w[k], w)
                planes.append(w * y_rows)
            xy_rows = jnp.concatenate(planes, 0)
            z_rows = split(dense_rows(corners[2:3], z_w, nz))
            target = [first[3 + k : 4 + k] for k in range(3)]
            spring = first[6:7]
            disp = [second[3 + k : 4 + k] for k in range(3)]
        along = dot3(flat, z_rows, ((1,), (0,)))
        cells = nx * ny
        partial = [
            jnp.sum(along[k * cells : (k + 1) * cells] * xy_rows, 0, keepdims=True)
            for k in range(3)
        ]
        velsum[step, me] = jnp.concatenate(partial, 1)
        sent += to_all(velsum.at[step], vel_s.at[step], vel_r.at[step])

        speed = velocity[0] * velocity[0] + velocity[1] * velocity[1] + velocity[2] * velocity[2]
        scaled = density * (1.0 / RELAX)
        base = scaled * (1.0 - 1.5 * speed)
        rest = source[0]
        post[step, SLOT[0]] = jnp.where(fluid, keep * rest + WEIGHTS[0] * base, rest)
        for i, j in PAIRS:
            proj = signed_sum(i, velocity)
            flow = scaled * proj
            even = WEIGHTS[i] * (base + 4.5 * flow * proj)
            odd = (3.0 * WEIGHTS[i]) * flow
            a, b = source[i], source[j]
            post[step, SLOT[i]] = jnp.where(fluid, keep * a + (even + odd), b)
            post[step, SLOT[j]] = jnp.where(fluid, keep * b + (even - odd), a)

        all_here(velsum.at[step], vel_s.at[step], vel_r.at[step])
        summed = velsum[step, 0]
        for s in range(1, n_sub):
            summed = summed + velsum[step, s]
        moved = [summed[:, k * total : (k + 1) * total] for k in range(3)]
        force = [KAPPA * (target[k] - moved[k]) - spring * disp[k] for k in range(3)]
        disp = [disp[k] + moved[k] for k in range(3)]
        weighted = split(jnp.concatenate([xy_rows * force[k] for k in range(3)], 0))
        spread = dot3(weighted, z_rows, ((1,), (1,))).reshape(3, nx, ny, nz)
        spread = [jnp.where(fluid, spread[k], 0.0) for k in range(3)]
        for i, j in PAIRS:
            push = (3.0 * WEIGHTS[i]) * signed_sum(i, spread)
            post[step, SLOT[i]] = post[step, SLOT[i]] + push
            post[step, SLOT[j]] = post[step, SLOT[j]] - push

        for n, i in enumerate(Y_UP):
            y_send[step, 0, n] = post[step, SLOT[i], :, ny - 1 : ny, :]
        for n, i in enumerate(Y_DN):
            y_send[step, 1, n] = post[step, SLOT[i], :, 0:1, :]
        for n, i in enumerate(EDGES):
            x = nx - 1 if DIRS[i][0] == 1 else 0
            y = ny - 1 if DIRS[i][1] == 1 else 0
            e_send[step, n] = post[step, SLOT[i], x, y : y + 1, :]
        ends = [
            (post.at[step, pl.ds(0, len(X_UP)), nx - 1], x_recv.at[step, 0]),
            (post.at[step, pl.ds(len(X_UP), len(X_DN)), 0], x_recv.at[step, 1]),
            (y_send.at[step, 0], y_recv.at[step, 0]),
            (y_send.at[step, 1], y_recv.at[step, 1]),
        ] + [(e_send.at[step, n], e_recv.at[step, n]) for n in range(len(EDGES))]
        halo = []
        for n, ((src, dst), (a, b)) in enumerate(zip(ends, targets)):
            copy = pltpu.make_async_remote_copy(
                src_ref=src,
                dst_ref=dst,
                send_sem=halo_s.at[step, n],
                recv_sem=halo_r.at[step, n],
                device_id=at(a, b),
                device_id_type=MESH,
            )
            copy.start()
            halo.append(copy)
        sent += halo

        dest = mid if step < STEPS - 1 else out_ref
        for i, (dx, dy, dz) in enumerate(DIRS):
            cells_i = post[step, SLOT[i]]
            if dx:
                cells_i = cells_i[: nx - 1] if dx == 1 else cells_i[1:]
            if dy:
                cells_i = pltpu.roll(cells_i, dy % ny, 1)
            if dz:
                cells_i = pltpu.roll(cells_i, dz % nz, 2)
            dest[i, pl.ds(max(dx, 0), nx - abs(dx))] = cells_i
        for copy in halo:
            copy.wait_recv()
        for i, (dx, dy, dz) in enumerate(DIRS):
            if dx:
                side, names = (0, X_UP) if dx == 1 else (1, X_DN)
                face = x_recv[step, side, names.index(i)]
                if dy:
                    face = pltpu.roll(face, dy % ny, 0)
                if dz:
                    face = pltpu.roll(face, dz % nz, 1)
                dest[i, 0 if dx == 1 else nx - 1] = face
            if dy:
                side, names = (0, Y_UP) if dy == 1 else (1, Y_DN)
                edge = y_recv[step, side, names.index(i)]
                if dx == 1:
                    edge = jnp.concatenate(
                        [e_recv[step, EDGES.index(i)][None], edge[: nx - 1]], 0
                    )
                elif dx == -1:
                    edge = jnp.concatenate([edge[1:], e_recv[step, EDGES.index(i)][None]], 0)
                if dz:
                    edge = pltpu.roll(edge.reshape(nx, nz), dz % nz, 1).reshape(nx, 1, nz)
                y = 0 if dy == 1 else ny - 1
                dest[i, :, y : y + 1, :] = edge

    for values, result in ((disp, disp_out), (force, force_out)):
        for k in range(3):
            mine = jnp.zeros((1, lanes), jnp.float32)
            for pair in range(n_sub // 2):
                part = values[k][:, pair * lanes : (pair + 1) * lanes]
                mine = jnp.where(me // 2 == pair, part, mine)
            mine = jnp.where(lax.rem(me, 2) == 0, mine, pltpu.roll(mine, count, 1))
            result[k : k + 1, :] = mine[:, :count]
    for copy in sent:
        copy.wait_send()


def shards(n_plate, n_sub, populations, solid, corner, frac, target, stiffness, displacement):
    _, nx, ny, nz = populations.shape
    count = stiffness.shape[0]
    f32 = jnp.float32
    vmem = pl.BlockSpec(memory_space=pltpu.VMEM)
    total = count * n_sub
    faces = len(X_UP)
    return pl.pallas_call(
        functools.partial(body, n_plate, n_sub),
        out_shape=(
            jax.ShapeDtypeStruct(populations.shape, f32),
            jax.ShapeDtypeStruct(displacement.shape, f32),
            jax.ShapeDtypeStruct(displacement.shape, f32),
        ),
        in_specs=[pl.BlockSpec(memory_space=pltpu.HBM)] * 7,
        out_specs=(vmem,) * 3,
        scratch_shapes=[
            pltpu.VMEM(populations.shape, f32),
            pltpu.VMEM(solid.shape, jnp.int32),
            pltpu.VMEM(corner.shape, jnp.int32),
            pltpu.VMEM(frac.shape, f32),
            pltpu.VMEM(target.shape, f32),
            pltpu.VMEM((1, count), f32),
            pltpu.VMEM(displacement.shape, f32),
            pltpu.VMEM((n_sub, 8, 2 * count), f32),
            pltpu.VMEM((STEPS, n_sub, 1, 3 * total), f32),
            pltpu.VMEM((STEPS, 19, nx, ny, nz), f32),
            pltpu.VMEM((19, nx, ny, nz), f32),
            pltpu.VMEM((STEPS, 2, faces, ny, nz), f32),
            pltpu.VMEM((STEPS, 2, faces, nx, 1, nz), f32),
            pltpu.VMEM((STEPS, 2, faces, nx, 1, nz), f32),
            pltpu.VMEM((STEPS, len(EDGES), 1, nz), f32),
            pltpu.VMEM((STEPS, len(EDGES), 1, nz), f32),
            pltpu.VMEM((8, 2 * count), f32),
            pltpu.SemaphoreType.DMA((n_sub,)),
            pltpu.SemaphoreType.DMA((n_sub,)),
            pltpu.SemaphoreType.DMA((STEPS, n_sub)),
            pltpu.SemaphoreType.DMA((STEPS, n_sub)),
            pltpu.SemaphoreType.DMA((STEPS, 8)),
            pltpu.SemaphoreType.DMA((STEPS, 8)),
            pltpu.SemaphoreType.DMA((7,)),
        ],
        compiler_params=pltpu.CompilerParams(
            collective_id=0, has_side_effects=True, vmem_limit_bytes=62 * 1024 * 1024
        ),
    )(populations, solid, corner, frac, target, stiffness[None], displacement)


def solution(mesh):
    in_specs = (
        P(None, "plate", "sub", None),
        P("plate", "sub", None),
        P(None, ("plate", "sub")),
        P(None, ("plate", "sub")),
        P(None, ("plate", "sub")),
        P(("plate", "sub")),
        P(None, ("plate", "sub")),
    )
    out_specs = (
        P(None, "plate", "sub", None),
        P(None, ("plate", "sub")),
        P(None, ("plate", "sub")),
    )
    run = functools.partial(shards, mesh.shape["plate"], mesh.shape["sub"])
    return jax.shard_map(run, mesh=mesh, in_specs=in_specs, out_specs=out_specs, check_vma=False)
```

```python
import functools

import jax
import jax.numpy as jnp
from jax import lax
from jax.experimental import pallas as pl
from jax.experimental.pallas import tpu as pltpu
from jax.sharding import PartitionSpec as P

STEPS = 2
DIRS = [
    (0, 0, 0),
    (1, 0, 0),
    (-1, 0, 0),
    (0, 1, 0),
    (0, -1, 0),
    (0, 0, 1),
    (0, 0, -1),
    (1, 1, 0),
    (-1, -1, 0),
    (1, -1, 0),
    (-1, 1, 0),
    (1, 0, 1),
    (-1, 0, -1),
    (1, 0, -1),
    (-1, 0, 1),
    (0, 1, 1),
    (0, -1, -1),
    (0, 1, -1),
    (0, -1, 1),
]
WEIGHTS = [1.0 / 3.0] + [1.0 / 18.0] * 6 + [1.0 / 36.0] * 12
PAIRS = [(i, i + 1) for i in range(1, 19, 2)]
KAPPA = 4.0
RELAX = 0.9
PIECES = 4
MESH = pl.DeviceIdType.MESH

X_UP = [i for i in range(19) if DIRS[i][0] == 1]
X_DN = [i for i in range(19) if DIRS[i][0] == -1]
Y_UP = [i for i in range(19) if DIRS[i][1] == 1]
Y_DN = [i for i in range(19) if DIRS[i][1] == -1]
EDGES = [i for i in range(19) if DIRS[i][0] and DIRS[i][1]]
ORDER = X_UP + X_DN + [i for i in range(19) if DIRS[i][0] == 0]
SLOT = [ORDER.index(i) for i in range(19)]


def signed_sum(index, vectors):
    total = None
    for axis in range(3):
        sign = DIRS[index][axis]
        if sign == 0:
            continue
        if total is None:
            total = vectors[axis] if sign == 1 else -vectors[axis]
        else:
            total = total + vectors[axis] if sign == 1 else total - vectors[axis]
    return total


def kernel_weights(frac):
    root = jnp.sqrt(1.0 + 4.0 * frac - 4.0 * frac * frac)
    second = (3.0 - 2.0 * frac + root) / 8.0
    third = (1.0 + 2.0 * frac + root) / 8.0
    return (0.5 - third, second, third, 0.5 - second)


def dense_rows(first, weights, length):
    cells = lax.broadcasted_iota(jnp.int32, (length, first.shape[1]), 0)
    offset = cells - first
    result = jnp.zeros(offset.shape, jnp.float32)
    for k in range(4):
        result = jnp.where(offset == k, weights[k], result)
    return result


def split(x):
    high = x.astype(jnp.bfloat16)
    return high, (x - high.astype(jnp.float32)).astype(jnp.bfloat16)


def dot3(a, b, dims):
    dot = functools.partial(
        lax.dot_general, dimension_numbers=(dims, ((), ())), preferred_element_type=jnp.float32
    )
    return dot(a[0], b[0]) + dot(a[1], b[0]) + dot(a[0], b[1])


def body(
    n_plate,
    n_sub,
    pops_hbm,
    solid_hbm,
    corner_hbm,
    frac_hbm,
    target_hbm,
    stiff_hbm,
    disp_hbm,
    out_ref,
    disp_out,
    force_out,
    pops_ref,
    solid_ref,
    corner_ref,
    frac_ref,
    target_ref,
    stiff_ref,
    disp_ref,
    marks,
    velsum,
    post,
    mid,
    x_recv,
    y_send,
    y_recv,
    e_send,
    e_recv,
    own,
    mark_s,
    mark_r,
    vel_s,
    vel_r,
    halo_s,
    halo_r,
    local,
):
    _, nx, ny, nz = pops_ref.shape
    count = frac_ref.shape[1]
    lanes = 2 * count
    plate, me = lax.axis_index("plate"), lax.axis_index("sub")

    def at(d_plate, d_sub):
        return (lax.rem(plate + d_plate + n_plate, n_plate), lax.rem(me + d_sub + n_sub, n_sub))

    targets = [(1, 0), (-1, 0), (0, 1), (0, -1)]
    greeted = {(0, k) for k in range(1, n_sub)}
    greeted |= {(a % n_plate, b % n_sub) for a, b in targets}
    greeted = sorted(greeted)
    barrier = pltpu.get_barrier_semaphore()
    for a, b in greeted:
        pl.semaphore_signal(barrier, inc=1, device_id=at(a, b), device_id_type=MESH)

    loads = [
        pltpu.make_async_copy(src, dst, local.at[n])
        for n, (src, dst) in enumerate(
            (
                (corner_hbm, corner_ref),
                (disp_hbm, disp_ref),
                (frac_hbm, frac_ref),
                (target_hbm, target_ref),
                (stiff_hbm, stiff_ref),
                (pops_hbm, pops_ref),
                (solid_hbm, solid_ref),
            )
        )
    ]
    for load in loads:
        load.start()
    for load in loads[:5]:
        load.wait()

    right_half = jnp.zeros((8, lanes), jnp.float32)
    own[...] = right_half
    own[0:3, 0:count] = corner_ref[...].astype(jnp.float32)
    own[3:6, 0:count] = disp_ref[...]
    right_half = pltpu.roll(own[...], count, 1)
    own[0:3, 0:count] = frac_ref[...]
    own[3:6, 0:count] = target_ref[...]
    own[6:7, 0:count] = stiff_ref[...]
    left = lax.broadcasted_iota(jnp.int32, (8, lanes), 1) < count
    marks[me] = jnp.where(left, own[...], right_half)

    pl.semaphore_wait(barrier, len(greeted))

    def to_all(buffer, send, recv):
        copies = []
        for k in range(1, n_sub):
            copy = pltpu.make_async_remote_copy(
                src_ref=buffer.at[me],
                dst_ref=buffer.at[me],
                send_sem=send.at[k],
                recv_sem=recv.at[k],
                device_id=at(0, k),
                device_id_type=MESH,
            )
            copy.start()
            copies.append(copy)
        return copies

    def all_here(buffer, send, recv):
        for k in range(1, n_sub):
            slot = lax.rem(me - k + n_sub, n_sub)
            pltpu.make_async_remote_copy(
                src_ref=buffer.at[slot],
                dst_ref=buffer.at[slot],
                send_sem=send.at[k],
                recv_sem=recv.at[k],
                device_id=at(0, k),
                device_id_type=MESH,
            ).wait_recv()

    def remote(step, n, src, dst, offsets):
        copy = pltpu.make_async_remote_copy(
            src_ref=src,
            dst_ref=dst,
            send_sem=halo_s.at[step, n],
            recv_sem=halo_r.at[step, n],
            device_id=at(*offsets),
            device_id_type=MESH,
        )
        copy.start()
        return copy

    ends = [[i for i in EDGES if DIRS[i][0] == sign] for sign in (1, -1)]
    sent = to_all(marks, mark_s, mark_r)

    def moments(pops):
        density = pops[0]
        for i in range(1, 19):
            density = density + pops[i]
        comps = []
        for axis in range(3):
            total = jnp.zeros_like(density)
            for i in range(19):
                if DIRS[i][axis] == 1:
                    total = total + pops[i]
                elif DIRS[i][axis] == -1:
                    total = total - pops[i]
            comps.append(total)
        inverse = 1.0 / density
        return density, [c * inverse for c in comps]

    for load in loads[5:]:
        load.wait()
    fluid = solid_ref[...] == 0
    mask = jnp.where(fluid, 1.0, 0.0)
    keep = 1.0 - 1.0 / RELAX
    disp = None
    for step in range(STEPS):
        source = pops_ref if step == 0 else mid
        density, velocity = moments([source[i] for i in range(19)])
        flat = split(jnp.concatenate(velocity, 0).reshape(3 * nx * ny, nz))
        if step == 0:
            all_here(marks, mark_s, mark_r)
            firsts, seconds = [], []
            for pair in range(n_sub // 2):
                a, b = marks[2 * pair], marks[2 * pair + 1]
                firsts.append(jnp.where(left, a, pltpu.roll(b, count, 1)))
                seconds.append(jnp.where(left, pltpu.roll(a, count, 1), b))
            first, second = jnp.concatenate(firsts, 1), jnp.concatenate(seconds, 1)
            total = first.shape[1]
            corners = second[0:3].astype(jnp.int32)
            x_first = corners[0:1] - plate * nx
            y_first = corners[1:2] - me * ny
            x_w, y_w, z_w = [kernel_weights(first[k : k + 1]) for k in range(3)]
            y_rows = dense_rows(y_first, y_w, ny)
            planes = []
            for x in range(nx):
                w = jnp.zeros_like(x_w[0])
                for k in range(4):
                    w = jnp.where(x_first == x - k, x_w[k], w)
                planes.append(w * y_rows)
            outside = []
            for y in (lax.rem(me + n_sub - 1, n_sub) * ny + ny - 1, lax.rem(me + 1, n_sub) * ny):
                y_row = jnp.zeros_like(y_w[0])
                for k in range(4):
                    y_row = jnp.where(corners[1:2] == y - k, y_w[k], y_row)
                for x in range(nx):
                    w = jnp.zeros_like(x_w[0])
                    for k in range(4):
                        w = jnp.where(x_first == x - k, x_w[k], w)
                    outside.append(w * y_row)
            xy_rows = jnp.concatenate(planes, 0)
            xy_outside = jnp.concatenate(outside, 0)
            z_rows = split(dense_rows(corners[2:3], z_w, nz))
            target = [first[3 + k : 4 + k] for k in range(3)]
            spring = first[6:7]
            disp = [second[3 + k : 4 + k] for k in range(3)]
        along = dot3(flat, z_rows, ((1,), (0,)))
        cells = nx * ny
        partial = [
            jnp.sum(along[k * cells : (k + 1) * cells] * xy_rows, 0, keepdims=True)
            for k in range(3)
        ]
        velsum[step, me] = jnp.concatenate(partial, 1)
        sent += to_all(velsum.at[step], vel_s.at[step], vel_r.at[step])

        speed = velocity[0] * velocity[0] + velocity[1] * velocity[1] + velocity[2] * velocity[2]
        scaled = density * (1.0 / RELAX)
        base = scaled * (1.0 - 1.5 * speed)
        rest = source[0]
        post[step, SLOT[0]] = jnp.where(fluid, keep * rest + WEIGHTS[0] * base, rest)
        for i, j in PAIRS:
            proj = signed_sum(i, velocity)
            flow = scaled * proj
            even = WEIGHTS[i] * (base + 4.5 * flow * proj)
            odd = (3.0 * WEIGHTS[i]) * flow
            a, b = source[i], source[j]
            post[step, SLOT[i]] = jnp.where(fluid, keep * a + (even + odd), b)
            post[step, SLOT[j]] = jnp.where(fluid, keep * b + (even - odd), a)

        for side, (names, y) in enumerate(((Y_UP, ny - 1), (Y_DN, 0))):
            for n, i in enumerate(names):
                y_send[step, side, n] = post[step, SLOT[i], :, y : y + 1, :]
            y_send[step, side, len(names)] = mask[:, y : y + 1, :]
        early = [
            remote(step, 2 + side, y_send.at[step, side], y_recv.at[step, side], targets[2 + side])
            for side in range(2)
        ]

        all_here(velsum.at[step], vel_s.at[step], vel_r.at[step])
        summed = velsum[step, 0]
        for s in range(1, n_sub):
            summed = summed + velsum[step, s]
        moved = [summed[:, k * total : (k + 1) * total] for k in range(3)]
        force = [KAPPA * (target[k] - moved[k]) - spring * disp[k] for k in range(3)]
        disp = [disp[k] + moved[k] for k in range(3)]
        rows = [xy_rows * force[k] for k in range(3)] + [xy_outside * force[k] for k in range(3)]
        everywhere = dot3(split(jnp.concatenate(rows, 0)), z_rows, ((1,), (1,)))
        spread = everywhere[: 3 * cells].reshape(3, nx, ny, nz)
        beyond = everywhere[3 * cells :].reshape(3, 2, nx, 1, nz)
        spread = [jnp.where(fluid, spread[k], 0.0) for k in range(3)]
        for i, j in PAIRS:
            push = (3.0 * WEIGHTS[i]) * signed_sum(i, spread)
            post[step, SLOT[i]] = post[step, SLOT[i]] + push
            post[step, SLOT[j]] = post[step, SLOT[j]] - push

        halo = [
            remote(step, 0, post.at[step, pl.ds(0, len(X_UP)), nx - 1], x_recv.at[step, 0], (1, 0)),
            remote(
                step, 1, post.at[step, pl.ds(len(X_UP), len(X_DN)), 0], x_recv.at[step, 1], (-1, 0)
            ),
        ]
        for copy in early:
            copy.wait_recv()
        edges = {}
        for side, names in enumerate((Y_UP, Y_DN)):
            wet = y_recv[step, side, len(names)]
            pushed = [beyond[k, side] * wet for k in range(3)]
            for n, i in enumerate(names):
                edges[i] = y_recv[step, side, n] + (3.0 * WEIGHTS[i]) * signed_sum(i, pushed)
        for side, sign in enumerate((1, -1)):
            for n, i in enumerate(ends[side]):
                e_send[step, side, n] = edges[i][nx - 1 if sign == 1 else 0]
            halo.append(
                remote(step, 4 + side, e_send.at[step, side], e_recv.at[step, side], (sign, 0))
            )
        sent += early + halo

        dest = mid if step < STEPS - 1 else out_ref
        for i, (dx, dy, dz) in enumerate(DIRS):
            cells_i = post[step, SLOT[i]]
            if dx:
                cells_i = cells_i[: nx - 1] if dx == 1 else cells_i[1:]
            if dy:
                cells_i = pltpu.roll(cells_i, dy % ny, 1)
            if dz:
                cells_i = pltpu.roll(cells_i, dz % nz, 2)
            dest[i, pl.ds(max(dx, 0), nx - abs(dx))] = cells_i
        for copy in halo:
            copy.wait_recv()
        for i, (dx, dy, dz) in enumerate(DIRS):
            if dx:
                side, names = (0, X_UP) if dx == 1 else (1, X_DN)
                face = x_recv[step, side, names.index(i)]
                if dy:
                    face = pltpu.roll(face, dy % ny, 0)
                if dz:
                    face = pltpu.roll(face, dz % nz, 1)
                dest[i, 0 if dx == 1 else nx - 1] = face
            if dy:
                edge = edges[i]
                if dx:
                    side = 0 if dx == 1 else 1
                    corner = e_recv[step, side, ends[side].index(i)][None]
                    parts = [corner, edge[: nx - 1]] if dx == 1 else [edge[1:], corner]
                    edge = jnp.concatenate(parts, 0)
                if dz:
                    edge = pltpu.roll(edge.reshape(nx, nz), dz % nz, 1).reshape(nx, 1, nz)
                y = 0 if dy == 1 else ny - 1
                dest[i, :, y : y + 1, :] = edge

    for values, result in ((disp, disp_out), (force, force_out)):
        for k in range(3):
            mine = jnp.zeros((1, lanes), jnp.float32)
            for pair in range(n_sub // 2):
                part = values[k][:, pair * lanes : (pair + 1) * lanes]
                mine = jnp.where(me // 2 == pair, part, mine)
            mine = jnp.where(lax.rem(me, 2) == 0, mine, pltpu.roll(mine, count, 1))
            result[k : k + 1, :] = mine[:, :count]
    for copy in sent:
        copy.wait_send()


def write_out(pops, disp, force, pops_out, disp_out, force_out, sems):
    count = pops.shape[0]
    cuts = [count * k // PIECES for k in range(PIECES + 1)]
    pairs = [(disp, disp_out), (force, force_out)]
    for low, high in zip(cuts, cuts[1:]):
        part = pl.ds(low, high - low)
        pairs.append((pops.at[part], pops_out.at[part]))
    copies = [
        pltpu.make_async_copy(src, dst, sems.at[n]) for n, (src, dst) in enumerate(pairs)
    ]
    for copy in copies:
        copy.start()
    for copy in copies:
        copy.wait()


def shards(n_plate, n_sub, populations, solid, corner, frac, target, stiffness, displacement):
    _, nx, ny, nz = populations.shape
    count = stiffness.shape[0]
    f32 = jnp.float32
    vmem = pl.BlockSpec(memory_space=pltpu.VMEM)
    total = count * n_sub
    faces = len(X_UP)
    results = (
        jax.ShapeDtypeStruct(populations.shape, f32),
        jax.ShapeDtypeStruct(displacement.shape, f32),
        jax.ShapeDtypeStruct(displacement.shape, f32),
    )
    values = pl.pallas_call(
        functools.partial(body, n_plate, n_sub),
        out_shape=results,
        in_specs=[pl.BlockSpec(memory_space=pltpu.HBM)] * 7,
        out_specs=(vmem,) * 3,
        scratch_shapes=[
            pltpu.VMEM(populations.shape, f32),
            pltpu.VMEM(solid.shape, jnp.int32),
            pltpu.VMEM(corner.shape, jnp.int32),
            pltpu.VMEM(frac.shape, f32),
            pltpu.VMEM(target.shape, f32),
            pltpu.VMEM((1, count), f32),
            pltpu.VMEM(displacement.shape, f32),
            pltpu.VMEM((n_sub, 8, 2 * count), f32),
            pltpu.VMEM((STEPS, n_sub, 1, 3 * total), f32),
            pltpu.VMEM((STEPS, 19, nx, ny, nz), f32),
            pltpu.VMEM((19, nx, ny, nz), f32),
            pltpu.VMEM((STEPS, 2, faces, ny, nz), f32),
            pltpu.VMEM((STEPS, 2, faces + 1, nx, 1, nz), f32),
            pltpu.VMEM((STEPS, 2, faces + 1, nx, 1, nz), f32),
            pltpu.VMEM((STEPS, 2, len(EDGES) // 2, 1, nz), f32),
            pltpu.VMEM((STEPS, 2, len(EDGES) // 2, 1, nz), f32),
            pltpu.VMEM((8, 2 * count), f32),
            pltpu.SemaphoreType.DMA((n_sub,)),
            pltpu.SemaphoreType.DMA((n_sub,)),
            pltpu.SemaphoreType.DMA((STEPS, n_sub)),
            pltpu.SemaphoreType.DMA((STEPS, n_sub)),
            pltpu.SemaphoreType.DMA((STEPS, 6)),
            pltpu.SemaphoreType.DMA((STEPS, 6)),
            pltpu.SemaphoreType.DMA((7,)),
        ],
        compiler_params=pltpu.CompilerParams(
            collective_id=0, has_side_effects=True, vmem_limit_bytes=62 * 1024 * 1024
        ),
    )(populations, solid, corner, frac, target, stiffness[None], displacement)
    return pl.pallas_call(
        write_out,
        out_shape=results,
        in_specs=[vmem] * 3,
        out_specs=(pl.BlockSpec(memory_space=pltpu.HBM),) * 3,
        scratch_shapes=[pltpu.SemaphoreType.DMA((PIECES + 2,))],
    )(*values)


def solution(mesh):
    in_specs = (
        P(None, "plate", "sub", None),
        P("plate", "sub", None),
        P(None, ("plate", "sub")),
        P(None, ("plate", "sub")),
        P(None, ("plate", "sub")),
        P(("plate", "sub")),
        P(None, ("plate", "sub")),
    )
    out_specs = (
        P(None, "plate", "sub", None),
        P(None, ("plate", "sub")),
        P(None, ("plate", "sub")),
    )
    run = functools.partial(shards, mesh.shape["plate"], mesh.shape["sub"])
    return jax.shard_map(run, mesh=mesh, in_specs=in_specs, out_specs=out_specs, check_vma=False)
```
